32 devices in a mesh: blocks: 32 (over z, y, x, core).
Axes of the slice: x: 2, y: 2, z: 4, core: 2. Of those that a mesh axis runs over, the one named last changes fastest.
Arguments:
- features: bfloat16 [192, 512, 128], P('blocks'), may hold values from -6 to 6
- cotangent: bfloat16 [192, 512, 128], P('blocks'), may hold values from -6 to 6
- weight_one: bfloat16 [27, 128, 128], replicated, may hold values from -0.109375 to 0.109375
- weight_two: bfloat16 [27, 128, 128], replicated, may hold values from -0.109375 to 0.109375
- occupancy: int32 [192, 512], P('blocks'), may hold values 0 or 1
- neighbours: int32 [192, 26], P('blocks'), may hold values from -1 to 191, as said below
Outputs:
- output: bfloat16 [192, 512, 128], P('blocks')
- grad_features: bfloat16 [192, 512, 128], P('blocks')
- grad_one: float32 [27, 128, 128], replicated
- grad_two: float32 [27, 128, 128], replicated
The draws below stay inside these ranges and needn't reach their ends.
Inputs may be any that keep to these rules, and one draw needn't show every extreme that they name: `neighbours`: the blocks are positions of a grid with one plane of the first coordinate a device: the first coordinate of a block is its device index. The link is symmetric (block q is p's neighbour at offset o exactly when p is q's at minus o). A neighbour at an offset whose first component is -1, 0 or +1 lies on the device before, the same device or the device after, respectively. The blocks of one device are in row-major order of their second and third coordinates.
All inputs are finite; a program needn't handle non-finite values. No bound on the sum of `occupancy` on one device may be relied on, other than what follows from the above.
Results may differ from the reference program's by a relative error of at most 0.0049.
Values may be sent and summed in bfloat16 or wider, within the bound.
A program may use at most 64 MiB of HBM per device.

```python
import jax
import jax.numpy as jnp
from jax import lax

C = 128
BLK_DEV = 6
BLOCKS = 192


def draw_neighbours(key, part):
    key = jax.random.fold_in(key, 11)
    planes = BLOCKS // BLK_DEV
    spots = 2 * BLK_DEV
    plane_keys = jax.random.split(key, planes)
    chosen = jax.vmap(lambda k: jnp.sort(jax.random.permutation(k, spots)[:BLK_DEV]))(plane_keys)
    chosen = chosen.astype(jnp.int32)
    slot_ids = jnp.arange(planes * BLK_DEV, dtype=jnp.int32).reshape(planes, BLK_DEV)
    plane_ids = jnp.arange(planes, dtype=jnp.int32)
    lookup = jnp.full((planes, spots), -1, jnp.int32)
    lookup = lookup.at[plane_ids[:, None], chosen].set(slot_ids)
    pos_x = jnp.repeat(plane_ids, BLK_DEV)
    flat_pos = chosen.reshape(-1)
    pos_y = flat_pos // BLK_DEV
    pos_z = flat_pos % BLK_DEV
    found_links = []
    for offset in range(27):
        if offset == 13:
            continue
        near_x = pos_x + (offset // 9 - 1)
        near_y = pos_y + (offset // 3 % 3 - 1)
        near_z = pos_z + (offset % 3 - 1)
        inside = (near_x >= 0) & (near_x < planes) & (near_y >= 0) & (near_y < 2) & (near_z >= 0) & (near_z < BLK_DEV)
        found = lookup[jnp.clip(near_x, 0, planes - 1), jnp.clip(near_y, 0, 1) * BLK_DEV + jnp.clip(near_z, 0, BLK_DEV - 1)]
        found_links.append(jnp.where(inside, found, -1))
    return jnp.stack(found_links, axis=1).astype(jnp.int32)


def plant(result, own_key, least, high):
    extent = result.shape
    index_at = [jax.random.randint(jax.random.fold_in(own_key, axis), (), 0, extent[axis]) for axis in range(len(extent))]
    result = result.at[tuple(index_at)].set(least)
    longest = extent.index(max(extent))
    index_at[longest] = (index_at[longest] + 1) % extent[longest]
    return result.at[tuple(index_at)].set(high)


def steps_of(key, shape, shards, smallest, largest):
    gain, own = 1.0, jax.random.fold_in(key, 6)
    for position, blocks in shards:
        steps = jnp.exp(jax.random.uniform(jax.random.fold_in(own, position), (blocks,), jnp.float32, smallest / len(shards), largest / len(shards)))
        gain = gain * jnp.repeat(steps, shape[position] // blocks).reshape([-1 if axis == position else 1 for axis in range(len(shape))])
    return gain


def centred(key, shape, scale, reach, cuts=(), kind=jnp.bfloat16):
    entries = scale * jax.random.normal(key, shape, jnp.float32)
    if cuts:
        entries = entries * steps_of(key, shape, cuts, -0.22, 0.18)
    return jnp.clip(entries, -reach, reach).astype(kind)


def setup_inputs(seed: int = 0) -> dict:
    streams_of = jax.random.split(jax.random.key(seed), 7)
    features = centred(streams_of[0], (BLOCKS, 512, C), 1.0, 6.0, ((0, 32),))
    cotangent = centred(streams_of[1], (BLOCKS, 512, C), 1.0, 6.0, ((0, 32),))
    weight_one = centred(streams_of[2], (27, C, C), (27 * C) ** -0.5, 0.109375)
    weight_two = centred(streams_of[3], (27, C, C), (27 * C) ** -0.5, 0.109375)
    occupancy = plant((jax.random.randint(streams_of[4], (BLOCKS, 512), 0, 2) < 1).astype(jnp.int32), jax.random.fold_in(streams_of[4], 1), 0, 1)
    neighbours = draw_neighbours(jax.random.fold_in(streams_of[6], 71), 0)
    return {"features": features, "cotangent": cotangent, "weight_one": weight_one, "weight_two": weight_two, "occupancy": occupancy, "neighbours": neighbours}


SPAN_TABLE = ((7, 8, 0), (0, 8, 1), (0, 1, 9))

def pad_tiles(own_tiles, source, local_links):
    channels = own_tiles.shape[-1]
    padded = jnp.zeros((own_tiles.shape[0], 10, 10, 10, channels), own_tiles.dtype)
    column = 0
    for offset in range(27):
        span_x = SPAN_TABLE[offset // 9]
        span_y = SPAN_TABLE[offset // 3 % 3]
        span_z = SPAN_TABLE[offset % 3]
        if offset == 13:
            portion = own_tiles
        else:
            link_col = local_links[:, column]
            column += 1
            region = source[:, span_x[0]:span_x[1], span_y[0]:span_y[1], span_z[0]:span_z[1], :]
            portion = jnp.take(region, jnp.maximum(link_col, 0).astype(jnp.int32), axis=0)
            present = (link_col >= 0)[:, None, None, None, None]
            portion = jnp.where(present, portion, jnp.zeros((), own_tiles.dtype))
        padded = padded.at[:, span_x[2]:span_x[2] + span_x[1] - span_x[0], span_y[2]:span_y[2] + span_y[1] - span_y[0], span_z[2]:span_z[2] + span_z[1] - span_z[0], :].set(portion)
    return padded

def columns(tile_pad):
    shifted = [tile_pad[a:a + 8, b:b + 8, c:c + 8, :] for a in range(3) for b in range(3) for c in range(3)]
    return jnp.concatenate(shifted, axis=-1).reshape(512, -1)

def conv_blocks(padded, weight_flat):

    def per_tile(tile_pad):
        return jnp.dot(columns(tile_pad), weight_flat, preferred_element_type=jnp.float32)
    return lax.map(per_tile, padded)

def weight_grad(padded, grads):
    channels = grads.shape[-1]

    def accumulate(running, paired):
        tile_pad, grad_tile = paired
        term = lax.dot_general(columns(tile_pad), grad_tile, (((0,), (0,)), ((), ())), preferred_element_type=jnp.float32)
        return (running + term, None)
    start_sum = jnp.zeros((27 * channels, channels), jnp.float32)
    running, _ = lax.scan(accumulate, start_sum, (padded, grads))
    return running.reshape(27, channels, channels)

def flat_weight(weight):
    return weight.reshape(-1, weight.shape[-1])

def flipped(weight):
    return weight[::-1].transpose(0, 2, 1).reshape(-1, weight.shape[-1])

def reference(features, cotangent, weight_one, weight_two, occupancy, neighbours):
    block_count, voxels, channels = features.shape
    mask_half = occupancy.astype(jnp.bfloat16)[..., None]
    mask_full = occupancy.astype(jnp.float32)[..., None]

    def spread(flat_rows):
        tile_view = flat_rows.reshape(block_count, 8, 8, 8, channels)
        return pad_tiles(tile_view, tile_view, neighbours)
    masked = features * mask_half
    pad_in = spread(masked)
    pre_act = conv_blocks(pad_in, flat_weight(weight_one)) * mask_full
    activation = (jax.nn.gelu(pre_act) * mask_full).astype(jnp.bfloat16)
    pad_act = spread(activation)
    output = (conv_blocks(pad_act, flat_weight(weight_two)) * mask_full).astype(jnp.bfloat16)
    grad_out = cotangent * mask_half
    pad_grad = spread(grad_out)
    grad_act = conv_blocks(pad_grad, flipped(weight_two)) * mask_full
    grad_two = weight_grad(pad_act, grad_out)
    slope = jax.vjp(jax.nn.gelu, pre_act)[1](grad_act)[0]
    grad_pre = (slope * mask_full).astype(jnp.bfloat16)
    pad_pre = spread(grad_pre)
    grad_features = (conv_blocks(pad_pre, flipped(weight_one)) * mask_full).astype(jnp.bfloat16)
    grad_one = weight_grad(pad_in, grad_pre)
    return (output, grad_features, grad_one, grad_two)
```

```python
import functools

import jax
import jax.numpy as jnp
from jax import lax
from jax.experimental import pallas as pl
from jax.experimental.pallas import tpu as pltpu
from jax.sharding import PartitionSpec as P

ROOT = 0.7978845608028654
CUBE = 0.044715
F32, BF16 = jnp.float32, jnp.bfloat16


def mm(left, right):
    return jnp.dot(left, right, preferred_element_type=F32)


def fill_columns(cols, own, prev, after, slots, count):
    z = lax.broadcasted_iota(jnp.int32, (10, 8, 128), 1)

    def one_block(blk, _):
        for p in range(10):
            dx = 0 if p == 0 else 2 if p == 9 else 1

            def rows(b, c, lo, hi):
                slot = slots[blk, dx * 9 + b * 3 + c]
                if dx == 0:
                    part = prev[slot, lo:hi]
                elif dx == 2:
                    part = after[slot, lo:hi]
                else:
                    part = own[slot, p - 1, lo:hi]
                return part.astype(F32)

            lines = [
                jnp.concatenate(
                    [rows(0, c, 48, 64)[8:], rows(1, c, 0, 64), rows(2, c, 0, 16)[:8]], axis=0
                ).reshape(10, 8, 128)
                for c in range(3)
            ]
            shifted = [
                pltpu.roll(jnp.where(z == 7, lines[0], lines[1]), 1, 1),
                lines[1],
                pltpu.roll(jnp.where(z == 0, lines[2], lines[1]), 7, 1),
            ]
            for b in range(3):
                for c in range(3):
                    at = (b * 3 + c) * 128
                    cols[p % 2, p // 2, blk, :, at : at + 128] = (
                        shifted[c][b : b + 8].reshape(64, 128).astype(BF16)
                    )
        return 0

    lax.fori_loop(0, count, one_block, 0)


def fill_weights(wide, weight, flip):
    for a in range(3):
        for t in range(9):
            o = a * 9 + t
            tap = weight[26 - o].T if flip else weight[o]
            for pair, half in ((0, 0), (1, 1)) if a == 1 else ((0, 1),) if a == 0 else ((1, 0),):
                wide[pair, t * 128 : t * 128 + 128, half * 128 : half * 128 + 128] = tap


def conv_step(cols, wide, q, count):
    rows = count * 64
    part = lambda par, at: cols[par, at].reshape(rows, 1152)
    both = mm(part(1, q), wide[0]) + mm(part(0, q + 1), wide[1])
    even = both[:, :128] + mm(part(0, q), wide[0, :, 128:])
    odd = both[:, 128:] + mm(part(1, q + 1), wide[1, :, :128])
    return even, odd


def pad_halo(dst, src, count):
    dst[:count] = src
    dst[count] = jnp.zeros((64, 128), BF16)


def front_kernel(
    count, slots, feat, cot, mask, prev_f, prev_c, next_f, next_c, w1, w2,
    act, gpre, g1, g2,
    own_f, own_c, pf, pc, nf, nc, cols_f, cols_c, wide1, wide2, act_t, gpre_t,
):
    own_f[:count] = feat[...] * mask[...]
    own_c[:count] = cot[...] * mask[...]
    own_f[count] = jnp.zeros((8, 64, 128), BF16)
    own_c[count] = jnp.zeros((8, 64, 128), BF16)
    for dst, src in ((pf, prev_f), (pc, prev_c), (nf, next_f), (nc, next_c)):
        pad_halo(dst, src[...], count)
    fill_weights(wide1, w1, False)
    fill_weights(wide2, w2, True)
    fill_columns(cols_f, own_f, pf, nf, slots, count)
    fill_columns(cols_c, own_c, pc, nc, slots, count)
    rows = count * 64

    def step(q, _):
        pres = conv_step(cols_f, wide1, q, count)
        grads = conv_step(cols_c, wide2, q, count)
        for par in range(2):
            gate = mask[:, 2 * q + par].reshape(rows, 128).astype(F32)
            x = pres[par] * gate
            t = jnp.tanh(ROOT * (x + CUBE * (x * x * x)))
            cdf = 0.5 * (1.0 + t)
            slope = cdf + x * (0.5 * (1.0 - t * t)) * (ROOT * (1.0 + (3.0 * CUBE) * (x * x)))
            a = (x * cdf * gate).astype(BF16)
            g = (grads[par] * gate * slope).astype(BF16)
            act[:, 2 * q + par] = a.reshape(count, 64, 128)
            gpre[:, 2 * q + par] = g.reshape(count, 64, 128)
            act_t[q, par * 128 : par * 128 + 128] = a.T
            gpre_t[q, par * 128 : par * 128 + 128] = g.T
        return 0

    lax.fori_loop(0, 4, step, 0)

    for b in range(3):
        for cols, left, out, flip in ((cols_f, gpre_t, g1, False), (cols_c, act_t, g2, True)):
            part = lambda par, at, q: cols[par, at + q, :, :, b * 384 : b * 384 + 384].reshape(rows, 384)
            total = lambda par, at, lo, hi: sum(
                mm(left[q, lo:hi], part(par, at, q)) for q in range(4)
            )
            r1 = total(1, 0, 0, 256)
            r2 = total(0, 1, 0, 256)
            sums = (
                total(0, 0, 0, 128) + r1[128:],
                r1[:128] + r2[128:],
                r2[:128] + total(1, 1, 128, 256),
            )
            for a in range(3):
                for c in range(3):
                    o = a * 9 + b * 3 + c
                    tile = sums[a][:, c * 128 : c * 128 + 128]
                    if flip:
                        out[26 - o] = tile
                    else:
                        out[o] = tile.T


def back_kernel(
    count, slots, act, gpre, mask, prev_f, prev_c, next_f, next_c, w1, w2,
    out, gfeat,
    own_f, own_c, pf, pc, nf, nc, cols_f, cols_c, wide1, wide2,
):
    own_f[:count] = act[...]
    own_c[:count] = gpre[...]
    own_f[count] = jnp.zeros((8, 64, 128), BF16)
    own_c[count] = jnp.zeros((8, 64, 128), BF16)
    for dst, src in ((pf, prev_f), (pc, prev_c), (nf, next_f), (nc, next_c)):
        pad_halo(dst, src[...], count)
    fill_weights(wide1, w1, True)
    fill_weights(wide2, w2, False)
    fill_columns(cols_f, own_f, pf, nf, slots, count)
    fill_columns(cols_c, own_c, pc, nc, slots, count)
    rows = count * 64

    def step(q, _):
        outs = conv_step(cols_f, wide2, q, count)
        grads = conv_step(cols_c, wide1, q, count)
        for par in range(2):
            gate = mask[:, 2 * q + par].reshape(rows, 128).astype(F32)
            out[:, 2 * q + par] = (outs[par] * gate).astype(BF16).reshape(count, 64, 128)
            gfeat[:, 2 * q + par] = (grads[par] * gate).astype(BF16).reshape(count, 64, 128)
        return 0

    lax.fori_loop(0, 4, step, 0)


def shards(features, cotangent, weight_one, weight_two, occupancy, neighbours):
    count = features.shape[0]
    shape = (count, 8, 64, 128)
    peers = lax.axis_size("blocks")
    me = lax.axis_index("blocks")
    ups = [(i, i + 1) for i in range(peers - 1)]
    downs = [(i + 1, i) for i in range(peers - 1)]
    mask = jnp.broadcast_to(occupancy.astype(BF16).reshape(count, 8, 64, 1), shape)
    feat = features.reshape(shape)
    cot = cotangent.reshape(shape)
    own = jnp.broadcast_to(me * count + jnp.arange(count, dtype=jnp.int32)[:, None], (count, 1))
    links = jnp.concatenate([neighbours[:, :13], own, neighbours[:, 13:]], axis=1)
    base = (me + jnp.arange(27, dtype=jnp.int32) // 9 - 1) * count
    slots = jnp.where(links >= 0, links - base[None], count).astype(jnp.int32)

    def swap(first, second, gate):
        lows = [first[:, 0], second[:, 0]]
        highs = [first[:, 7], second[:, 7]]
        if gate is not None:
            lows = [v * gate[:, 0] for v in lows]
            highs = [v * gate[:, 7] for v in highs]
        before = lax.ppermute(jnp.stack(highs), "blocks", ups)
        after = lax.ppermute(jnp.stack(lows), "blocks", downs)
        return before[0], before[1], after[0], after[1]

    smem = pl.BlockSpec(memory_space=pltpu.SMEM)
    vmem = pl.BlockSpec(memory_space=pltpu.VMEM)
    padded = [pltpu.VMEM((count + 1, 8, 64, 128), BF16)] * 2 + [
        pltpu.VMEM((count + 1, 64, 128), BF16)
    ] * 4
    cols = [pltpu.VMEM((2, 5, count, 64, 1152), BF16)] * 2
    wides = [pltpu.VMEM((2, 1152, 256), BF16)] * 2
    params = pltpu.CompilerParams(vmem_limit_bytes=58 * 1024 * 1024)
    field = jax.ShapeDtypeStruct(shape, BF16)
    grad = jax.ShapeDtypeStruct((27, 128, 128), F32)
    act, gpre, g1, g2 = pl.pallas_call(
        functools.partial(front_kernel, count),
        out_shape=(field, field, grad, grad),
        in_specs=[smem] + [vmem] * 9,
        out_specs=(vmem,) * 4,
        scratch_shapes=padded + cols + wides + [pltpu.VMEM((4, 256, count * 64), BF16)] * 2,
        compiler_params=params,
        cost_estimate=pl.CostEstimate(flops=11 * 10**9, bytes_accessed=10**7, transcendentals=400000),
        name="front",
    )(slots, feat, cot, mask, *swap(feat, cot, mask), weight_one, weight_two)
    grad_one, grad_two = lax.psum((g1, g2), "blocks")
    out, gfeat = pl.pallas_call(
        functools.partial(back_kernel, count),
        out_shape=(field, field),
        in_specs=[smem] + [vmem] * 9,
        out_specs=(vmem,) * 2,
        scratch_shapes=padded + cols + wides,
        compiler_params=params,
        cost_estimate=pl.CostEstimate(flops=6 * 10**9, bytes_accessed=10**7, transcendentals=0),
        name="back",
    )(slots, act, gpre, mask, *swap(act, gpre, None), weight_one, weight_two)
    return (
        out.reshape(features.shape),
        gfeat.reshape(features.shape),
        grad_one,
        grad_two,
    )


def solution(mesh):
    return jax.shard_map(
        shards,
        mesh=mesh,
        in_specs=(
            P("blocks", None, None),
            P("blocks", None, None),
            P(),
            P(),
            P("blocks", None),
            P("blocks", None),
        ),
        out_specs=(P("blocks", None, None), P("blocks", None, None), P(), P()),
        check_vma=False,
    )
```

```python
import functools

import jax
import jax.numpy as jnp
from jax import lax
from jax.experimental import pallas as pl
from jax.experimental.pallas import tpu as pltpu
from jax.sharding import PartitionSpec as P

ROOT = 0.7978845608028654
CUBE = 0.044715
F32, BF16 = jnp.float32, jnp.bfloat16


def mm(left, right):
    return jnp.dot(left, right, preferred_element_type=F32)


def fill_columns(cols, own, prev, after, slots, count):
    z = lax.broadcasted_iota(jnp.int32, (10, 8, 128), 1)

    def one_block(blk, _):
        for p in range(10):
            dx = 0 if p == 0 else 2 if p == 9 else 1

            def rows(b, c, lo, hi):
                slot = slots[blk, dx * 9 + b * 3 + c]
                if dx == 0:
                    part = prev[slot, lo:hi]
                elif dx == 2:
                    part = after[slot, lo:hi]
                else:
                    part = own[slot, p - 1, lo:hi]
                return part.astype(F32)

            lines = [
                jnp.concatenate(
                    [rows(0, c, 48, 64)[8:], rows(1, c, 0, 64), rows(2, c, 0, 16)[:8]], axis=0
                ).reshape(10, 8, 128)
                for c in range(3)
            ]
            shifted = [
                pltpu.roll(jnp.where(z == 7, lines[0], lines[1]), 1, 1),
                lines[1],
                pltpu.roll(jnp.where(z == 0, lines[2], lines[1]), 7, 1),
            ]
            for b in range(3):
                for c in range(3):
                    at = (b * 3 + c) * 128
                    cols[p % 2, p // 2, blk, :, at : at + 128] = (
                        shifted[c][b : b + 8].reshape(64, 128).astype(BF16)
                    )
        return 0

    lax.fori_loop(0, count, one_block, 0)


def fill_weights(wide, weight, flip):
    for a in range(3):
        for t in range(9):
            o = a * 9 + t
            tap = weight[26 - o].T if flip else weight[o]
            for pair, half in ((0, 0), (1, 1)) if a == 1 else ((0, 1),) if a == 0 else ((1, 0),):
                wide[pair, t * 128 : t * 128 + 128, half * 128 : half * 128 + 128] = tap


def conv_step(cols, wide, q, count):
    rows = count * 64
    part = lambda par, at: cols[par, at].reshape(rows, 1152)
    both = mm(part(1, q), wide[0]) + mm(part(0, q + 1), wide[1])
    even = both[:, :128] + mm(part(0, q), wide[0, :, 128:])
    odd = both[:, 128:] + mm(part(1, q + 1), wide[1, :, :128])
    return even, odd


def pad_halo(dst, src, count):
    dst[:count] = src
    dst[count] = jnp.zeros((64, 128), BF16)


def front_kernel(
    count, slots, feat, cot, mask, prev_f, prev_c, next_f, next_c, w1, w2,
    act, gpre, grads_out,
    own_f, own_c, pf, pc, nf, nc, cols_f, cols_c, wide1, wide2, act_t, gpre_t,
):
    own_f[:count] = feat[...] * mask[...]
    own_c[:count] = cot[...] * mask[...]
    own_f[count] = jnp.zeros((8, 64, 128), BF16)
    own_c[count] = jnp.zeros((8, 64, 128), BF16)
    for dst, src in ((pf, prev_f), (pc, prev_c), (nf, next_f), (nc, next_c)):
        pad_halo(dst, src[...], count)
    fill_weights(wide1, w1, False)
    fill_weights(wide2, w2, True)
    fill_columns(cols_f, own_f, pf, nf, slots, count)
    fill_columns(cols_c, own_c, pc, nc, slots, count)
    rows = count * 64

    def step(q, _):
        pres = conv_step(cols_f, wide1, q, count)
        grads = conv_step(cols_c, wide2, q, count)
        for par in range(2):
            gate = mask[:, 2 * q + par].reshape(rows, 128).astype(F32)
            x = pres[par] * gate
            t = jnp.tanh(ROOT * (x + CUBE * (x * x * x)))
            cdf = 0.5 * (1.0 + t)
            slope = cdf + x * (0.5 * (1.0 - t * t)) * (ROOT * (1.0 + (3.0 * CUBE) * (x * x)))
            a = (x * cdf * gate).astype(BF16)
            g = (grads[par] * gate * slope).astype(BF16)
            act[:, 2 * q + par] = a.reshape(count, 64, 128)
            gpre[:, 2 * q + par] = g.reshape(count, 64, 128)
            act_t[q, par * 128 : par * 128 + 128] = a.T
            gpre_t[q, par * 128 : par * 128 + 128] = g.T
        return 0

    lax.fori_loop(0, 4, step, 0)

    for b in range(3):
        for cols, left, flip in ((cols_f, gpre_t, False), (cols_c, act_t, True)):
            part = lambda par, at, q: cols[par, at + q, :, :, b * 384 : b * 384 + 384].reshape(rows, 384)
            total = lambda par, at, lo, hi: sum(
                mm(left[q, lo:hi], part(par, at, q)) for q in range(4)
            )
            r1 = total(1, 0, 0, 256)
            r2 = total(0, 1, 0, 256)
            sums = (
                total(0, 0, 0, 128) + r1[128:],
                r1[:128] + r2[128:],
                r2[:128] + total(1, 1, 128, 256),
            )
            for a in range(3):
                for c in range(3):
                    o = a * 9 + b * 3 + c
                    tile = sums[a][:, c * 128 : c * 128 + 128]
                    tap = 53 - o if flip else o
                    at = tap % 18 * 128
                    grads_out[tap // 18, at : at + 128] = tile if flip else tile.T
    for part in range(3):
        spare = grads_out.shape[1] - 2304
        grads_out[part, 2304:] = jnp.zeros((spare, 128), F32)


def sum_steps(peers, grads, total, outbox, inbox, result, sems):
    me = lax.axis_index("blocks")
    bits = peers.bit_length() - 1
    send, recv, send_all, recv_all = sems
    orders, lows, signs = [], [], []
    for part in range(3):
        turn = part * (bits - 1) // 3
        rest = list(range(1, bits))
        order = [0] + rest[turn:] + rest[:turn]
        low, lo, sign = 0, [0], []
        for s, k in enumerate(order):
            bit = me // 2**k % 2
            low = low + bit * (peers >> (s + 1))
            lo.append(low)
            sign.append(bit)
        orders.append(order)
        lows.append(lo)
        signs.append(sign)

    def partner(part, s):
        return me + 2 ** orders[part][s] * (1 - 2 * signs[part][s])

    def halve(part, s):
        half = peers >> (s + 1)
        other = lows[part][s] + (1 - signs[part][s]) * half
        at = peers - (peers >> s)
        return other, half, at, pltpu.make_async_remote_copy(
            src_ref=outbox.at[part, pl.ds(other, half)],
            dst_ref=inbox.at[part, pl.ds(at, half)],
            send_sem=send.at[part, s],
            recv_sem=recv.at[part, s],
            device_id=(partner(part, s),),
            device_id_type=pl.DeviceIdType.MESH,
        )

    def double(part, s):
        held = pl.ds(lows[part][s + 1], peers >> (s + 1))
        return pltpu.make_async_remote_copy(
            src_ref=result.at[part, held],
            dst_ref=result.at[part, held],
            send_sem=send_all.at[part, s],
            recv_sem=recv_all.at[part, s],
            device_id=(partner(part, s),),
            device_id_type=pl.DeviceIdType.MESH,
        )

    def start_halve(s):
        source = grads if s == 0 else total
        for part in range(3):
            other, half, _, copy = halve(part, s)
            outbox[part, pl.ds(other, half)] = source[part, pl.ds(other, half)].astype(BF16)
            copy.start()

    def finish_halve(s):
        source = grads if s == 0 else total
        for part in range(3):
            _, half, at, copy = halve(part, s)
            copy.wait()
            mine = pl.ds(lows[part][s + 1], half)
            value = source[part, mine] + inbox[part, at : at + half].astype(F32)
            if s == bits - 1:
                result[part, mine] = value.astype(BF16)
            else:
                total[part, mine] = value

    def start_double(s):
        for part in range(3):
            double(part, s).start()

    def finish_double(s):
        for part in range(3):
            double(part, s).wait()

    steps = [(functools.partial(start_halve, s), functools.partial(finish_halve, s)) for s in range(bits)]
    steps += [
        (functools.partial(start_double, s), functools.partial(finish_double, s))
        for s in reversed(range(bits))
    ]
    return steps


def greet(peers):
    me = lax.axis_index("blocks")
    bits = peers.bit_length() - 1
    barrier = pltpu.get_barrier_semaphore()
    for k in range(bits):
        other = me + 2**k * (1 - 2 * (me // 2**k % 2))
        pl.semaphore_signal(barrier, inc=1, device_id=(other,), device_id_type=pl.DeviceIdType.MESH)
    pl.semaphore_wait(barrier, bits)


def sum_kernel(peers, grads, summed, total, outbox, inbox, result, *sems):
    greet(peers)
    for start, finish in sum_steps(peers, grads, total, outbox, inbox, result, sems):
        start()
        finish()
    summed[...] = result[...]


def back_kernel(
    count, slots, act, gpre, mask, prev_f, prev_c, next_f, next_c, w1, w2,
    out, gfeat,
    own_f, own_c, pf, pc, nf, nc, cols_f, cols_c, wide1, wide2,
):
    own_f[:count] = act[...]
    own_c[:count] = gpre[...]
    own_f[count] = jnp.zeros((8, 64, 128), BF16)
    own_c[count] = jnp.zeros((8, 64, 128), BF16)
    for dst, src in ((pf, prev_f), (pc, prev_c), (nf, next_f), (nc, next_c)):
        pad_halo(dst, src[...], count)
    fill_weights(wide1, w1, True)
    fill_weights(wide2, w2, False)
    fill_columns(cols_f, own_f, pf, nf, slots, count)
    fill_columns(cols_c, own_c, pc, nc, slots, count)
    rows = count * 64

    def step(q, _):
        outs = conv_step(cols_f, wide2, q, count)
        grads = conv_step(cols_c, wide1, q, count)
        for par in range(2):
            gate = mask[:, 2 * q + par].reshape(rows, 128).astype(F32)
            out[:, 2 * q + par] = (outs[par] * gate).astype(BF16).reshape(count, 64, 128)
            gfeat[:, 2 * q + par] = (grads[par] * gate).astype(BF16).reshape(count, 64, 128)
        return 0

    lax.fori_loop(0, 4, step, 0)


def shards(features, cotangent, weight_one, weight_two, occupancy, neighbours):
    count = features.shape[0]
    shape = (count, 8, 64, 128)
    peers = lax.axis_size("blocks")
    me = lax.axis_index("blocks")
    ups = [(i, i + 1) for i in range(peers - 1)]
    downs = [(i + 1, i) for i in range(peers - 1)]
    mask = jnp.broadcast_to(occupancy.astype(BF16).reshape(count, 8, 64, 1), shape)
    feat = features.reshape(shape)
    cot = cotangent.reshape(shape)
    own = jnp.broadcast_to(me * count + jnp.arange(count, dtype=jnp.int32)[:, None], (count, 1))
    links = jnp.concatenate([neighbours[:, :13], own, neighbours[:, 13:]], axis=1)
    base = (me + jnp.arange(27, dtype=jnp.int32) // 9 - 1) * count
    slots = jnp.where(links >= 0, links - base[None], count).astype(jnp.int32)

    def swap(first, second, gate):
        lows = [first[:, 0], second[:, 0]]
        highs = [first[:, 7], second[:, 7]]
        if gate is not None:
            lows = [v * gate[:, 0] for v in lows]
            highs = [v * gate[:, 7] for v in highs]
        before = lax.ppermute(jnp.stack(highs), "blocks", ups)
        after = lax.ppermute(jnp.stack(lows), "blocks", downs)
        return before[0], before[1], after[0], after[1]

    smem = pl.BlockSpec(memory_space=pltpu.SMEM)
    vmem = pl.BlockSpec(memory_space=pltpu.VMEM)
    padded = [pltpu.VMEM((count + 1, 8, 64, 128), BF16)] * 2 + [
        pltpu.VMEM((count + 1, 64, 128), BF16)
    ] * 4
    cols = [pltpu.VMEM((2, 5, count, 64, 1152), BF16)] * 2
    wides = [pltpu.VMEM((2, 1152, 256), BF16)] * 2
    params = pltpu.CompilerParams(vmem_limit_bytes=58 * 1024 * 1024)
    field = jax.ShapeDtypeStruct(shape, BF16)
    chunk = -(-2304 // (16 * peers)) * 16
    bits = peers.bit_length() - 1
    grad = jax.ShapeDtypeStruct((3, chunk * peers, 128), F32)
    act, gpre, grads = pl.pallas_call(
        functools.partial(front_kernel, count),
        out_shape=(field, field, grad),
        in_specs=[smem] + [vmem] * 9,
        out_specs=(vmem,) * 3,
        scratch_shapes=padded + cols + wides + [pltpu.VMEM((4, 256, count * 64), BF16)] * 2,
        compiler_params=params,
        cost_estimate=pl.CostEstimate(flops=11 * 10**9, bytes_accessed=10**7, transcendentals=400000),
        name="front",
    )(slots, feat, cot, mask, *swap(feat, cot, mask), weight_one, weight_two)
    pieces = (3, peers, chunk, 128)
    bridge = [pltpu.VMEM(pieces, F32)] + [pltpu.VMEM(pieces, BF16)] * 3
    bridge += [pltpu.SemaphoreType.DMA((3, bits))] * 4
    summed = pl.pallas_call(
        functools.partial(sum_kernel, peers),
        out_shape=jax.ShapeDtypeStruct(pieces, BF16),
        in_specs=[vmem],
        out_specs=vmem,
        scratch_shapes=bridge,
        compiler_params=pltpu.CompilerParams(
            vmem_limit_bytes=58 * 1024 * 1024, collective_id=0, has_side_effects=True
        ),
        name="total",
    )(grads.reshape(pieces))
    summed = summed.reshape(3, chunk * peers, 128)[:, :2304].reshape(54, 128, 128).astype(F32)
    grad_one, grad_two = summed[:27], summed[27:]
    out, gfeat = pl.pallas_call(
        functools.partial(back_kernel, count),
        out_shape=(field, field),
        in_specs=[smem] + [vmem] * 9,
        out_specs=(vmem,) * 2,
        scratch_shapes=padded + cols + wides,
        compiler_params=params,
        cost_estimate=pl.CostEstimate(flops=6 * 10**9, bytes_accessed=10**7, transcendentals=0),
        name="back",
    )(slots, act, gpre, mask, *swap(act, gpre, None), weight_one, weight_two)
    return (
        out.reshape(features.shape),
        gfeat.reshape(features.shape),
        grad_one,
        grad_two,
    )


def solution(mesh):
    return jax.shard_map(
        shards,
        mesh=mesh,
        in_specs=(
            P("blocks", None, None),
            P("blocks", None, None),
            P(),
            P(),
            P("blocks", None),
            P("blocks", None),
        ),
        out_specs=(P("blocks", None, None), P("blocks", None, None), P(), P()),
        check_vma=False,
    )
```

```python
import functools

import jax
import jax.numpy as jnp
from jax import lax
from jax.experimental import pallas as pl
from jax.experimental.pallas import tpu as pltpu
from jax.sharding import PartitionSpec as P

ROOT = 0.7978845608028654
CUBE = 0.044715
F32, BF16 = jnp.float32, jnp.bfloat16


def mm(left, right):
    return jnp.dot(left, right, preferred_element_type=F32)


def fill_columns(cols, own, prev, after, slots, count):
    z = lax.broadcasted_iota(jnp.int32, (10, 8, 128), 1)

    def one_block(blk, _):
        for p in range(10):
            dx = 0 if p == 0 else 2 if p == 9 else 1

            def rows(b, c, lo, hi):
                slot = slots[blk, dx * 9 + b * 3 + c]
                if dx == 0:
                    part = prev[slot, lo:hi]
                elif dx == 2:
                    part = after[slot, lo:hi]
                else:
                    part = own[slot, p - 1, lo:hi]
                return part.astype(F32)

            lines = [
                jnp.concatenate(
                    [rows(0, c, 48, 64)[8:], rows(1, c, 0, 64), rows(2, c, 0, 16)[:8]], axis=0
                ).reshape(10, 8, 128)
                for c in range(3)
            ]
            shifted = [
                pltpu.roll(jnp.where(z == 7, lines[0], lines[1]), 1, 1),
                lines[1],
                pltpu.roll(jnp.where(z == 0, lines[2], lines[1]), 7, 1),
            ]
            for b in range(3):
                for c in range(3):
                    at = (b * 3 + c) * 128
                    cols[p % 2, p // 2, blk, :, at : at + 128] = (
                        shifted[c][b : b + 8].reshape(64, 128).astype(BF16)
                    )
        return 0

    lax.fori_loop(0, count, one_block, 0)


def fill_weights(wide, weight, flip):
    for a in range(3):
        for t in range(9):
            o = a * 9 + t
            tap = weight[26 - o].T if flip else weight[o]
            for pair, half in ((0, 0), (1, 1)) if a == 1 else ((0, 1),) if a == 0 else ((1, 0),):
                wide[pair, t * 128 : t * 128 + 128, half * 128 : half * 128 + 128] = tap


def conv_step(cols, wide, q, count):
    rows = count * 64
    part = lambda par, at: cols[par, at].reshape(rows, 1152)
    both = mm(part(1, q), wide[0]) + mm(part(0, q + 1), wide[1])
    even = both[:, :128] + mm(part(0, q), wide[0, :, 128:])
    odd = both[:, 128:] + mm(part(1, q + 1), wide[1, :, :128])
    return even, odd


def pad_halo(dst, src, count):
    dst[:count] = src
    dst[count] = jnp.zeros((64, 128), BF16)


def front_kernel(
    count, slots, feat, cot, mask, prev_f, prev_c, next_f, next_c, w1, w2,
    act, gpre, grads_out,
    own_f, own_c, pf, pc, nf, nc, cols_f, cols_c, wide1, wide2, act_t, gpre_t,
):
    own_f[:count] = feat[...] * mask[...]
    own_c[:count] = cot[...] * mask[...]
    own_f[count] = jnp.zeros((8, 64, 128), BF16)
    own_c[count] = jnp.zeros((8, 64, 128), BF16)
    for dst, src in ((pf, prev_f), (pc, prev_c), (nf, next_f), (nc, next_c)):
        pad_halo(dst, src[...], count)
    fill_weights(wide1, w1, False)
    fill_weights(wide2, w2, True)
    fill_columns(cols_f, own_f, pf, nf, slots, count)
    fill_columns(cols_c, own_c, pc, nc, slots, count)
    rows = count * 64

    def step(q, _):
        pres = conv_step(cols_f, wide1, q, count)
        grads = conv_step(cols_c, wide2, q, count)
        for par in range(2):
            gate = mask[:, 2 * q + par].reshape(rows, 128).astype(F32)
            x = pres[par] * gate
            t = jnp.tanh(ROOT * (x + CUBE * (x * x * x)))
            cdf = 0.5 * (1.0 + t)
            slope = cdf + x * (0.5 * (1.0 - t * t)) * (ROOT * (1.0 + (3.0 * CUBE) * (x * x)))
            a = (x * cdf * gate).astype(BF16)
            g = (grads[par] * gate * slope).astype(BF16)
            act[:, 2 * q + par] = a.reshape(count, 64, 128)
            gpre[:, 2 * q + par] = g.reshape(count, 64, 128)
            act_t[q, par * 128 : par * 128 + 128] = a.T
            gpre_t[q, par * 128 : par * 128 + 128] = g.T
        return 0

    lax.fori_loop(0, 4, step, 0)

    for b in range(3):
        for cols, left, flip in ((cols_f, gpre_t, False), (cols_c, act_t, True)):
            part = lambda par, at, q: cols[par, at + q, :, :, b * 384 : b * 384 + 384].reshape(rows, 384)
            total = lambda par, at, lo, hi: sum(
                mm(left[q, lo:hi], part(par, at, q)) for q in range(4)
            )
            r1 = total(1, 0, 0, 256)
            r2 = total(0, 1, 0, 256)
            sums = (
                total(0, 0, 0, 128) + r1[128:],
                r1[:128] + r2[128:],
                r2[:128] + total(1, 1, 128, 256),
            )
            for a in range(3):
                for c in range(3):
                    o = a * 9 + b * 3 + c
                    tile = sums[a][:, c * 128 : c * 128 + 128]
                    tap = 53 - o if flip else o
                    at = tap % 18 * 128
                    grads_out[tap // 18, at : at + 128] = tile if flip else tile.T
    for part in range(3):
        spare = grads_out.shape[1] - 2304
        grads_out[part, 2304:] = jnp.zeros((spare, 128), F32)


def sum_steps(peers, grads, total, outbox, inbox, result, sems):
    me = lax.axis_index("blocks")
    bits = peers.bit_length() - 1
    send, recv, send_all, recv_all = sems
    orders, lows, signs = [], [], []
    for part in range(3):
        turn = part * (bits - 1) // 3
        rest = list(range(1, bits))
        order = [0] + rest[turn:] + rest[:turn]
        low, lo, sign = 0, [0], []
        for s, k in enumerate(order):
            bit = me // 2**k % 2
            low = low + bit * (peers >> (s + 1))
            lo.append(low)
            sign.append(bit)
        orders.append(order)
        lows.append(lo)
        signs.append(sign)

    def partner(part, s):
        return me + 2 ** orders[part][s] * (1 - 2 * signs[part][s])

    def halve(part, s):
        half = peers >> (s + 1)
        other = lows[part][s] + (1 - signs[part][s]) * half
        at = peers - (peers >> s)
        return other, half, at, pltpu.make_async_remote_copy(
            src_ref=outbox.at[part, pl.ds(other, half)],
            dst_ref=inbox.at[part, pl.ds(at, half)],
            send_sem=send.at[part, s],
            recv_sem=recv.at[part, s],
            device_id=(partner(part, s),),
            device_id_type=pl.DeviceIdType.MESH,
        )

    def double(part, s):
        held = pl.ds(lows[part][s + 1], peers >> (s + 1))
        return pltpu.make_async_remote_copy(
            src_ref=result.at[part, held],
            dst_ref=result.at[part, held],
            send_sem=send_all.at[part, s],
            recv_sem=recv_all.at[part, s],
            device_id=(partner(part, s),),
            device_id_type=pl.DeviceIdType.MESH,
        )

    def start_halve(s):
        source = grads if s == 0 else total
        for part in range(3):
            other, half, _, copy = halve(part, s)
            outbox[part, pl.ds(other, half)] = source[part, pl.ds(other, half)].astype(BF16)
            copy.start()

    def finish_halve(s):
        source = grads if s == 0 else total
        for part in range(3):
            _, half, at, copy = halve(part, s)
            copy.wait()
            mine = pl.ds(lows[part][s + 1], half)
            value = source[part, mine] + inbox[part, at : at + half].astype(F32)
            if s == bits - 1:
                result[part, mine] = value.astype(BF16)
            else:
                total[part, mine] = value

    def start_double(s):
        for part in range(3):
            double(part, s).start()

    def finish_double(s):
        for part in range(3):
            double(part, s).wait()

    steps = [(functools.partial(start_halve, s), functools.partial(finish_halve, s)) for s in range(bits)]
    steps += [
        (functools.partial(start_double, s), functools.partial(finish_double, s))
        for s in reversed(range(bits))
    ]
    return steps


def greet(peers):
    me = lax.axis_index("blocks")
    bits = peers.bit_length() - 1
    barrier = pltpu.get_barrier_semaphore()
    for k in range(bits):
        other = me + 2**k * (1 - 2 * (me // 2**k % 2))
        pl.semaphore_signal(barrier, inc=1, device_id=(other,), device_id_type=pl.DeviceIdType.MESH)
    for other in ((me + 1) % peers, (me + peers - 1) % peers):
        pl.semaphore_signal(barrier, inc=1, device_id=(other,), device_id_type=pl.DeviceIdType.MESH)
    pl.semaphore_wait(barrier, bits + 2)


def back_kernel(
    peers, count, slots, act, gpre, mask, w1, w2, grads,
    out, gfeat, summed,
    own_f, own_c, edges, halo, cols_f, cols_c, wide1, wide2,
    total, outbox, inbox, result, edge_send, edge_recv, *sems,
):
    greet(peers)
    me = lax.axis_index("blocks")
    rows = count * 64
    steps = sum_steps(peers, grads, total, outbox, inbox, result, sems)
    steps[0][0]()

    for i, (field, x) in enumerate(((act, 7), (gpre, 7), (act, 0), (gpre, 0))):
        edges[i, :count] = field[:, x]
        edges[i, count] = jnp.zeros((64, 128), BF16)
    swaps = []
    for i, other in enumerate(((me + 1) % peers, (me + peers - 1) % peers)):
        swaps.append(
            pltpu.make_async_remote_copy(
                src_ref=edges.at[pl.ds(2 * i, 2)],
                dst_ref=halo.at[pl.ds(2 * i, 2)],
                send_sem=edge_send.at[i],
                recv_sem=edge_recv.at[i],
                device_id=(other,),
                device_id_type=pl.DeviceIdType.MESH,
            )
        )
        swaps[i].start()

    def weights():
        own_f[:count] = act[...]
        own_c[:count] = gpre[...]
        own_f[count] = jnp.zeros((8, 64, 128), BF16)
        own_c[count] = jnp.zeros((8, 64, 128), BF16)
        fill_weights(wide1, w1, True)
        fill_weights(wide2, w2, False)

    def first_field():
        for swap in swaps:
            swap.wait()
        fill_columns(cols_f, own_f, halo.at[0], halo.at[2], slots, count)

    def second_field():
        fill_columns(cols_c, own_c, halo.at[1], halo.at[3], slots, count)

    def step(q, _):
        outs = conv_step(cols_f, wide2, q, count)
        grads = conv_step(cols_c, wide1, q, count)
        for par in range(2):
            gate = mask[:, 2 * q + par].reshape(rows, 128).astype(F32)
            out[:, 2 * q + par] = (outs[par] * gate).astype(BF16).reshape(count, 64, 128)
            gfeat[:, 2 * q + par] = (grads[par] * gate).astype(BF16).reshape(count, 64, 128)
        return 0

    bits = len(steps) // 2
    work = {
        0: weights,
        1: first_field,
        2: second_field,
        bits - 1: lambda: lax.fori_loop(0, 2, step, 0),
        2 * bits - 2: lambda: lax.fori_loop(2, 4, step, 0),
    }
    for n, (start, finish) in enumerate(steps):
        if n:
            start()
        if n in work:
            work[n]()
        finish()
    summed[...] = result[...]


def shards(features, cotangent, weight_one, weight_two, occupancy, neighbours):
    count = features.shape[0]
    shape = (count, 8, 64, 128)
    peers = lax.axis_size("blocks")
    me = lax.axis_index("blocks")
    ups = [(i, i + 1) for i in range(peers - 1)]
    downs = [(i + 1, i) for i in range(peers - 1)]
    mask = jnp.broadcast_to(occupancy.astype(BF16).reshape(count, 8, 64, 1), shape)
    feat = features.reshape(shape)
    cot = cotangent.reshape(shape)
    own = jnp.broadcast_to(me * count + jnp.arange(count, dtype=jnp.int32)[:, None], (count, 1))
    links = jnp.concatenate([neighbours[:, :13], own, neighbours[:, 13:]], axis=1)
    base = (me + jnp.arange(27, dtype=jnp.int32) // 9 - 1) * count
    slots = jnp.where(links >= 0, links - base[None], count).astype(jnp.int32)

    def swap(first, second, gate):
        lows = [first[:, 0] * gate[:, 0], second[:, 0] * gate[:, 0]]
        highs = [first[:, 7] * gate[:, 7], second[:, 7] * gate[:, 7]]
        before = lax.ppermute(jnp.stack(highs), "blocks", ups)
        after = lax.ppermute(jnp.stack(lows), "blocks", downs)
        return before[0], before[1], after[0], after[1]

    smem = pl.BlockSpec(memory_space=pltpu.SMEM)
    vmem = pl.BlockSpec(memory_space=pltpu.VMEM)
    padded = [pltpu.VMEM((count + 1, 8, 64, 128), BF16)] * 2 + [
        pltpu.VMEM((count + 1, 64, 128), BF16)
    ] * 4
    cols = [pltpu.VMEM((2, 5, count, 64, 1152), BF16)] * 2
    wides = [pltpu.VMEM((2, 1152, 256), BF16)] * 2
    params = pltpu.CompilerParams(vmem_limit_bytes=58 * 1024 * 1024)
    field = jax.ShapeDtypeStruct(shape, BF16)
    chunk = -(-2304 // (16 * peers)) * 16
    bits = peers.bit_length() - 1
    grad = jax.ShapeDtypeStruct((3, chunk * peers, 128), F32)
    act, gpre, grads = pl.pallas_call(
        functools.partial(front_kernel, count),
        out_shape=(field, field, grad),
        in_specs=[smem] + [vmem] * 9,
        out_specs=(vmem,) * 3,
        scratch_shapes=padded + cols + wides + [pltpu.VMEM((4, 256, count * 64), BF16)] * 2,
        compiler_params=params,
        cost_estimate=pl.CostEstimate(flops=11 * 10**9, bytes_accessed=10**7, transcendentals=400000),
        name="front",
    )(slots, feat, cot, mask, *swap(feat, cot, mask), weight_one, weight_two)
    pieces = (3, peers, chunk, 128)
    bridge = [pltpu.VMEM(pieces, F32)] + [pltpu.VMEM(pieces, BF16)] * 3
    bridge += [pltpu.SemaphoreType.DMA((3, bits))] * 4
    out, gfeat, summed = pl.pallas_call(
        functools.partial(back_kernel, peers, count),
        out_shape=(field, field, jax.ShapeDtypeStruct(pieces, BF16)),
        in_specs=[smem] + [vmem] * 6,
        out_specs=(vmem,) * 3,
        scratch_shapes=padded[:2]
        + [pltpu.VMEM((4, count + 1, 64, 128), BF16)] * 2
        + cols
        + wides
        + bridge[:4]
        + [pltpu.SemaphoreType.DMA((2,))] * 2
        + bridge[4:],
        compiler_params=pltpu.CompilerParams(
            vmem_limit_bytes=58 * 1024 * 1024, collective_id=0, has_side_effects=True
        ),
        name="back",
    )(slots, act, gpre, mask, weight_one, weight_two, grads.reshape(pieces))
    summed = summed.reshape(3, chunk * peers, 128)[:, :2304].reshape(54, 128, 128).astype(F32)
    grad_one, grad_two = summed[:27], summed[27:]
    return (
        out.reshape(features.shape),
        gfeat.reshape(features.shape),
        grad_one,
        grad_two,
    )


def solution(mesh):
    return jax.shard_map(
        shards,
        mesh=mesh,
        in_specs=(
            P("blocks", None, None),
            P("blocks", None, None),
            P(),
            P(),
            P("blocks", None),
            P("blocks", None),
        ),
        out_specs=(P("blocks", None, None), P("blocks", None, None), P(), P()),
        check_vma=False,
    )
```

```python
import functools

import jax
import jax.numpy as jnp
from jax import lax
from jax.experimental import pallas as pl
from jax.experimental.pallas import tpu as pltpu
from jax.sharding import PartitionSpec as P

ROOT = 0.7978845608028654
CUBE = 0.044715
F32, BF16 = jnp.float32, jnp.bfloat16


def mm(left, right):
    return jnp.dot(left, right, preferred_element_type=F32)


def fill_columns(cols, own, prev, after, slots, count):
    z = lax.broadcasted_iota(jnp.int32, (10, 8, 128), 1)

    def one_block(blk, _):
        for p in range(10):
            dx = 0 if p == 0 else 2 if p == 9 else 1

            def rows(b, c, lo, hi):
                slot = slots[blk, dx * 9 + b * 3 + c]
                if dx == 0:
                    part = prev[slot, lo:hi]
                elif dx == 2:
                    part = after[slot, lo:hi]
                else:
                    part = own[slot, p - 1, lo:hi]
                return part.astype(F32)

            lines = [
                jnp.concatenate(
                    [rows(0, c, 48, 64)[8:], rows(1, c, 0, 64), rows(2, c, 0, 16)[:8]], axis=0
                ).reshape(10, 8, 128)
                for c in range(3)
            ]
            shifted = [
                pltpu.roll(jnp.where(z == 7, lines[0], lines[1]), 1, 1),
                lines[1],
                pltpu.roll(jnp.where(z == 0, lines[2], lines[1]), 7, 1),
            ]
            for b in range(3):
                for c in range(3):
                    at = (b * 3 + c) * 128
                    cols[p % 2, p // 2, blk, :, at : at + 128] = (
                        shifted[c][b : b + 8].reshape(64, 128).astype(BF16)
                    )
        return 0

    lax.fori_loop(0, count, one_block, 0)


def fill_weights(wide, weight, flip):
    for a in range(3):
        for t in range(9):
            o = a * 9 + t
            tap = weight[26 - o].T if flip else weight[o]
            for pair, half in ((0, 0), (1, 1)) if a == 1 else ((0, 1),) if a == 0 else ((1, 0),):
                wide[pair, t * 128 : t * 128 + 128, half * 128 : half * 128 + 128] = tap


def conv_step(cols, wide, q, count):
    rows = count * 64
    part = lambda par, at: cols[par, at].reshape(rows, 1152)
    both = mm(part(1, q), wide[0]) + mm(part(0, q + 1), wide[1])
    even = both[:, :128] + mm(part(0, q), wide[0, :, 128:])
    odd = both[:, 128:] + mm(part(1, q + 1), wide[1, :, :128])
    return even, odd


def pad_halo(dst, src, count):
    dst[:count] = src
    dst[count] = jnp.zeros((64, 128), BF16)


def front_kernel(
    count, slots, feat, cot, mask, prev_f, prev_c, next_f, next_c, w1, w2,
    act, gpre, grads_out,
    own_f, own_c, pf, pc, nf, nc, cols_f, cols_c, wide1, wide2, act_t, gpre_t,
):
    own_f[:count] = feat[...] * mask[...]
    own_c[:count] = cot[...] * mask[...]
    own_f[count] = jnp.zeros((8, 64, 128), BF16)
    own_c[count] = jnp.zeros((8, 64, 128), BF16)
    for dst, src in ((pf, prev_f), (pc, prev_c), (nf, next_f), (nc, next_c)):
        pad_halo(dst, src[...], count)
    fill_weights(wide1, w1, False)
    fill_weights(wide2, w2, True)
    fill_columns(cols_f, own_f, pf, nf, slots, count)
    fill_columns(cols_c, own_c, pc, nc, slots, count)
    rows = count * 64

    def step(q, _):
        pres = conv_step(cols_f, wide1, q, count)
        grads = conv_step(cols_c, wide2, q, count)
        for par in range(2):
            gate = mask[:, 2 * q + par].reshape(rows, 128).astype(F32)
            x = pres[par] * gate
            t = jnp.tanh(ROOT * (x + CUBE * (x * x * x)))
            cdf = 0.5 * (1.0 + t)
            slope = cdf + x * (0.5 * (1.0 - t * t)) * (ROOT * (1.0 + (3.0 * CUBE) * (x * x)))
            a = (x * cdf * gate).astype(BF16)
            g = (grads[par] * gate * slope).astype(BF16)
            act[:, 2 * q + par] = a.reshape(count, 64, 128)
            gpre[:, 2 * q + par] = g.reshape(count, 64, 128)
            act_t[q, par * 128 : par * 128 + 128] = a.T
            gpre_t[q, par * 128 : par * 128 + 128] = g.T
        return 0

    lax.fori_loop(0, 4, step, 0)

    for b in range(3):
        for cols, left, flip in ((cols_f, gpre_t, False), (cols_c, act_t, True)):
            part = lambda par, at, q: cols[par, at + q, :, :, b * 384 : b * 384 + 384].reshape(rows, 384)
            total = lambda par, at, lo, hi: sum(
                mm(left[q, lo:hi], part(par, at, q)) for q in range(4)
            )
            r1 = total(1, 0, 0, 256)
            r2 = total(0, 1, 0, 256)
            sums = (
                total(0, 0, 0, 128) + r1[128:],
                r1[:128] + r2[128:],
                r2[:128] + total(1, 1, 128, 256),
            )
            for a in range(3):
                for c in range(3):
                    o = a * 9 + b * 3 + c
                    tile = sums[a][:, c * 128 : c * 128 + 128]
                    tap = 53 - o if flip else o
                    at = tap % 18 * 128
                    grads_out[tap // 18, at : at + 128] = tile if flip else tile.T
    for part in range(3):
        spare = grads_out.shape[1] - 2304
        grads_out[part, 2304:] = jnp.zeros((spare, 128), F32)


def sum_steps(peers, grads, total, outbox, inbox, result, sems):
    me = lax.axis_index("blocks")
    bits = peers.bit_length() - 1
    send, recv, send_all, recv_all = sems
    orders, lows, signs = [], [], []
    for part in range(3):
        turn = part * (bits - 1) // 3
        rest = list(range(1, bits))
        order = [0] + rest[turn:] + rest[:turn]
        low, lo, sign = 0, [0], []
        for s, k in enumerate(order):
            bit = me // 2**k % 2
            low = low + bit * (peers >> (s + 1))
            lo.append(low)
            sign.append(bit)
        orders.append(order)
        lows.append(lo)
        signs.append(sign)

    def partner(part, s):
        return me + 2 ** orders[part][s] * (1 - 2 * signs[part][s])

    def halve(part, s):
        half = peers >> (s + 1)
        other = lows[part][s] + (1 - signs[part][s]) * half
        at = peers - (peers >> s)
        return other, half, at, pltpu.make_async_remote_copy(
            src_ref=outbox.at[part, pl.ds(other, half)],
            dst_ref=inbox.at[part, pl.ds(at, half)],
            send_sem=send.at[part, s],
            recv_sem=recv.at[part, s],
            device_id=(partner(part, s),),
            device_id_type=pl.DeviceIdType.MESH,
        )

    def double(part, s):
        held = pl.ds(lows[part][s + 1], peers >> (s + 1))
        return pltpu.make_async_remote_copy(
            src_ref=result.at[part, held],
            dst_ref=result.at[part, held],
            send_sem=send_all.at[part, s],
            recv_sem=recv_all.at[part, s],
            device_id=(partner(part, s),),
            device_id_type=pl.DeviceIdType.MESH,
        )

    def start_halve(s, part):
        source = grads if s == 0 else total
        other, half, _, copy = halve(part, s)
        outbox[part, pl.ds(other, half)] = source[part, pl.ds(other, half)].astype(BF16)
        copy.start()

    def finish_halve(s, part):
        source = grads if s == 0 else total
        _, half, at, copy = halve(part, s)
        copy.wait()
        mine = pl.ds(lows[part][s + 1], half)
        value = source[part, mine] + inbox[part, at : at + half].astype(F32)
        if s == bits - 1:
            result[part, mine] = value.astype(BF16)
        else:
            total[part, mine] = value

    def start_double(s, part):
        double(part, s).start()

    def finish_double(s, part):
        double(part, s).wait()

    steps = [(functools.partial(start_halve, s), functools.partial(finish_halve, s)) for s in range(bits)]
    steps += [
        (functools.partial(start_double, s), functools.partial(finish_double, s))
        for s in reversed(range(bits))
    ]
    return steps


def greet(peers):
    me = lax.axis_index("blocks")
    bits = peers.bit_length() - 1
    barrier = pltpu.get_barrier_semaphore()
    for k in range(bits):
        other = me + 2**k * (1 - 2 * (me // 2**k % 2))
        pl.semaphore_signal(barrier, inc=1, device_id=(other,), device_id_type=pl.DeviceIdType.MESH)
    for other in ((me + 1) % peers, (me + peers - 1) % peers):
        pl.semaphore_signal(barrier, inc=1, device_id=(other,), device_id_type=pl.DeviceIdType.MESH)
    pl.semaphore_wait(barrier, bits + 2)


def back_kernel(
    peers, count, slots, act, gpre, mask, w1, w2, grads,
    out, gfeat, summed,
    own_f, own_c, edges, halo, cols_f, cols_c, wide1, wide2,
    total, outbox, inbox, result, edge_send, edge_recv, *sems,
):
    greet(peers)
    me = lax.axis_index("blocks")
    rows = count * 64
    steps = sum_steps(peers, grads, total, outbox, inbox, result, sems)
    for part in range(3):
        steps[0][0](part)

    for i, (field, x) in enumerate(((act, 7), (gpre, 7), (act, 0), (gpre, 0))):
        edges[i, :count] = field[:, x]
        edges[i, count] = jnp.zeros((64, 128), BF16)
    swaps = []
    for i, other in enumerate(((me + 1) % peers, (me + peers - 1) % peers)):
        swaps.append(
            pltpu.make_async_remote_copy(
                src_ref=edges.at[pl.ds(2 * i, 2)],
                dst_ref=halo.at[pl.ds(2 * i, 2)],
                send_sem=edge_send.at[i],
                recv_sem=edge_recv.at[i],
                device_id=(other,),
                device_id_type=pl.DeviceIdType.MESH,
            )
        )
        swaps[i].start()

    def weights():
        own_f[:count] = act[...]
        own_c[:count] = gpre[...]
        own_f[count] = jnp.zeros((8, 64, 128), BF16)
        own_c[count] = jnp.zeros((8, 64, 128), BF16)
        fill_weights(wide1, w1, True)
        fill_weights(wide2, w2, False)

    def first_field():
        for swap in swaps:
            swap.wait()
        fill_columns(cols_f, own_f, halo.at[0], halo.at[2], slots, count)

    def second_field():
        fill_columns(cols_c, own_c, halo.at[1], halo.at[3], slots, count)

    def step(q, _):
        outs = conv_step(cols_f, wide2, q, count)
        grads = conv_step(cols_c, wide1, q, count)
        for par in range(2):
            gate = mask[:, 2 * q + par].reshape(rows, 128).astype(F32)
            out[:, 2 * q + par] = (outs[par] * gate).astype(BF16).reshape(count, 64, 128)
            gfeat[:, 2 * q + par] = (grads[par] * gate).astype(BF16).reshape(count, 64, 128)
        return 0

    bits = len(steps) // 2
    work = {
        0: weights,
        1: first_field,
        2: second_field,
        bits - 1: lambda: lax.fori_loop(0, 2, step, 0),
        2 * bits - 2: lambda: lax.fori_loop(2, 4, step, 0),
    }
    for n, (_, finish) in enumerate(steps):
        if n in work:
            work[n]()
        for part in range(3):
            finish(part)
            if n + 1 < len(steps):
                steps[n + 1][0](part)
            else:
                summed[part] = result[part]


def shards(features, cotangent, weight_one, weight_two, occupancy, neighbours):
    count = features.shape[0]
    shape = (count, 8, 64, 128)
    peers = lax.axis_size("blocks")
    me = lax.axis_index("blocks")
    ups = [(i, i + 1) for i in range(peers - 1)]
    downs = [(i + 1, i) for i in range(peers - 1)]
    mask = jnp.broadcast_to(occupancy.astype(BF16).reshape(count, 8, 64, 1), shape)
    feat = features.reshape(shape)
    cot = cotangent.reshape(shape)
    own = jnp.broadcast_to(me * count + jnp.arange(count, dtype=jnp.int32)[:, None], (count, 1))
    links = jnp.concatenate([neighbours[:, :13], own, neighbours[:, 13:]], axis=1)
    base = (me + jnp.arange(27, dtype=jnp.int32) // 9 - 1) * count
    slots = jnp.where(links >= 0, links - base[None], count).astype(jnp.int32)

    def swap(first, second, gate):
        lows = [first[:, 0] * gate[:, 0], second[:, 0] * gate[:, 0]]
        highs = [first[:, 7] * gate[:, 7], second[:, 7] * gate[:, 7]]
        before = lax.ppermute(jnp.stack(highs), "blocks", ups)
        after = lax.ppermute(jnp.stack(lows), "blocks", downs)
        return before[0], before[1], after[0], after[1]

    smem = pl.BlockSpec(memory_space=pltpu.SMEM)
    vmem = pl.BlockSpec(memory_space=pltpu.VMEM)
    padded = [pltpu.VMEM((count + 1, 8, 64, 128), BF16)] * 2 + [
        pltpu.VMEM((count + 1, 64, 128), BF16)
    ] * 4
    cols = [pltpu.VMEM((2, 5, count, 64, 1152), BF16)] * 2
    wides = [pltpu.VMEM((2, 1152, 256), BF16)] * 2
    params = pltpu.CompilerParams(vmem_limit_bytes=58 * 1024 * 1024)
    field = jax.ShapeDtypeStruct(shape, BF16)
    chunk = -(-2304 // (16 * peers)) * 16
    bits = peers.bit_length() - 1
    grad = jax.ShapeDtypeStruct((3, chunk * peers, 128), F32)
    act, gpre, grads = pl.pallas_call(
        functools.partial(front_kernel, count),
        out_shape=(field, field, grad),
        in_specs=[smem] + [vmem] * 9,
        out_specs=(vmem,) * 3,
        scratch_shapes=padded + cols + wides + [pltpu.VMEM((4, 256, count * 64), BF16)] * 2,
        compiler_params=params,
        cost_estimate=pl.CostEstimate(flops=11 * 10**9, bytes_accessed=10**7, transcendentals=400000),
        name="front",
    )(slots, feat, cot, mask, *swap(feat, cot, mask), weight_one, weight_two)
    pieces = (3, peers, chunk, 128)
    bridge = [pltpu.VMEM(pieces, F32)] + [pltpu.VMEM(pieces, BF16)] * 3
    bridge += [pltpu.SemaphoreType.DMA((3, bits))] * 4
    out, gfeat, summed = pl.pallas_call(
        functools.partial(back_kernel, peers, count),
        out_shape=(field, field, jax.ShapeDtypeStruct(pieces, BF16)),
        in_specs=[smem] + [vmem] * 6,
        out_specs=(vmem,) * 3,
        scratch_shapes=padded[:2]
        + [pltpu.VMEM((4, count + 1, 64, 128), BF16)] * 2
        + cols
        + wides
        + bridge[:4]
        + [pltpu.SemaphoreType.DMA((2,))] * 2
        + bridge[4:],
        compiler_params=pltpu.CompilerParams(
            vmem_limit_bytes=58 * 1024 * 1024, collective_id=0, has_side_effects=True
        ),
        name="back",
    )(slots, act, gpre, mask, weight_one, weight_two, grads.reshape(pieces))
    summed = summed.reshape(3, chunk * peers, 128)[:, :2304].reshape(54, 128, 128).astype(F32)
    grad_one, grad_two = summed[:27], summed[27:]
    return (
        out.reshape(features.shape),
        gfeat.reshape(features.shape),
        grad_one,
        grad_two,
    )


def solution(mesh):
    return jax.shard_map(
        shards,
        mesh=mesh,
        in_specs=(
            P("blocks", None, None),
            P("blocks", None, None),
            P(),
            P(),
            P("blocks", None),
            P("blocks", None),
        ),
        out_specs=(P("blocks", None, None), P("blocks", None, None), P(), P()),
        check_vma=False,
    )
```
